32 devices in a mesh: pair: 8 (over y, x, core), cores: 4 (over z).
Axes of the slice: x: 2, y: 2, z: 4, core: 2. Of those that a mesh axis runs over, the one named last changes fastest.
Arguments:
- basis_rows: bfloat16 [16384, 2048], P('pair'), may hold values from -0.046875 to 0.046875
- energies: float32 [16384], P('pair'), may hold values from 0.5 to 4
- integrals: bfloat16 [16384, 4096], P('pair', 'cores'), may hold values from -0.75 to 0.75
- core_amps: bfloat16 [2048, 2048], P(('pair', 'cores')), may hold values from -3 to 3
- denominators: float32 [2048], replicated, may hold values from 1 to 4
Outputs:
- core_next: float32 [2048, 2048], P(('pair', 'cores'))
- amplitudes: bfloat16 [16384, 2048], P('pair')
The draws below stay inside these ranges and needn't reach their ends.
All inputs are finite; a program needn't handle non-finite values.
Results may differ from the reference program's by a relative error of at most 0.0056.
Values may be sent and summed in bfloat16 or wider, within the bound.
A program may use at most 128 MiB of HBM per device.

```python
import math
import jax
import jax.numpy as jnp

R = 2048
NAUX = 4096
NOV = 16384


def level_of(rng, shape, shards, least, top_value):
    def one(dim, parts):
        draws = jax.random.uniform(jax.random.fold_in(jax.random.fold_in(rng, 6), dim), (parts,), jnp.float32, least / len(shards), top_value / len(shards))
        return jnp.repeat(jnp.exp(draws), shape[dim] // parts).reshape((-1,) + (1,) * (len(shape) - dim - 1))

    factor_of = one(*shards[0])
    for cut in shards[1:]:
        factor_of = factor_of * one(*cut)
    return factor_of


def gaussian(rng, extent, width, bound, pieces=(), dtype=jnp.bfloat16):
    values = width * jax.random.normal(rng, extent, jnp.float32)
    if pieces:
        values = values * level_of(rng, extent, pieces, -0.22, 0.18)
    return jnp.clip(values, -bound, bound).astype(dtype)


def setup_inputs(seed: int = 0) -> dict:
    arg_keys = jax.random.split(jax.random.key(seed), 6)
    return {
        "basis_rows": gaussian(arg_keys[0], (NOV, R), NOV ** -0.5, 0.046875, ((0, 8),)),
        "energies": jnp.clip(jnp.exp(math.log(4.0) - 2.0794415 * jax.random.uniform(arg_keys[1], (NOV,), jnp.float32) ** level_of(arg_keys[1], (NOV,), ((0, 8),), -0.2, 0.2)), 0.5, 4.0),
        "integrals": gaussian(arg_keys[2], (NOV, NAUX), (NAUX ** 0.5) ** -0.5, 0.75, ((0, 8), (1, 4))),
        "core_amps": gaussian(arg_keys[3], (R, R), 0.5, 3.0, ((0, 32),)),
        "denominators": jnp.clip(jnp.exp(jax.random.uniform(arg_keys[4], (R,), jnp.float32, math.log(1.0), math.log(4.0))), 1.0, 4.0),
    }


def reference(basis_rows, energies, integrals, core_amps, denominators):
    projected = jnp.dot(basis_rows.T, integrals, preferred_element_type=jnp.float32)
    projected_b = projected.astype(jnp.bfloat16)
    coulomb = jnp.dot(projected_b, projected_b.T, preferred_element_type=jnp.float32)
    weighted = (energies[:, None] * basis_rows.astype(jnp.float32)).astype(jnp.bfloat16)
    fock = jnp.dot(weighted.T, basis_rows, preferred_element_type=jnp.float32)
    fock_b = fock.astype(jnp.bfloat16)
    residual = coulomb + jnp.dot(fock_b, core_amps, preferred_element_type=jnp.float32)
    core_next = core_amps.astype(jnp.float32) - residual / (denominators[:, None] + denominators[None, :])
    core_b = core_next.astype(jnp.bfloat16)
    amplitudes = jnp.dot(basis_rows, core_b, preferred_element_type=jnp.float32).astype(jnp.bfloat16)
    return core_next, amplitudes
```

```python
import functools

import jax
import jax.numpy as jnp
from jax import lax
from jax.experimental import pallas as pl
from jax.experimental.pallas import tpu as pltpu
from jax.sharding import PartitionSpec as P

F32 = jnp.float32
BF16 = jnp.bfloat16
MESH = pl.DeviceIdType.MESH


def dot_nn(left, right):
    return lax.dot_general(left, right, (((1,), (0,)), ((), ())), preferred_element_type=F32)


def dot_nt(left, right):
    return lax.dot_general(left, right, (((1,), (1,)), ((), ())), preferred_element_type=F32)


def one_hot(rows, columns, column_of):
    row = lax.broadcasted_iota(jnp.int32, (rows, columns), 0)
    column = lax.broadcasted_iota(jnp.int32, (rows, columns), 1)
    return jnp.where(column == column_of(row), 1.0, 0.0).astype(BF16)


def kernel(
    n, m, H,
    basis_hbm, energies, integrals_hbm, core_hbm, own_denoms, denoms,
    next_ref, amps_hbm,
    basis, ints, left, sib_out, sib_in, summed, peer_in, final, final_t, p_all, c_all,
    term, term_b, z_in, core_all, stage,
    load_sem, out_sem, c_send, c_fwd, c_recv, s_send, s_recv, x_send, x_recv,
    p_send, p_fwd, p_recv, z_send, z_recv, zg_send, g_send, g_fwd, g_recv,
):
    me, z = lax.axis_index("pair"), lax.axis_index("cores")
    nc = n // 2
    chip, c = me // 2, lax.rem(me, 2)
    sib = chip * 2 + 1 - c
    S, R = basis.shape
    A = ints.shape[1]
    K, blk = R // m, R // n
    o = blk // m
    w = R // H
    D = A + K
    TM = D // 3

    def peer(i):
        return lax.rem(chip + i, nc) * 2 + c

    def back(i):
        return lax.rem(chip + nc - i, nc) * 2 + c

    def other(i):
        return lax.rem(chip + nc - i, nc) * 2 + 1 - c

    def rc(src, dst, ssem, rsem, pair, zz):
        return pltpu.make_async_remote_copy(
            src_ref=src, dst_ref=dst, send_sem=ssem, recv_sem=rsem,
            device_id=(pair, zz), device_id_type=MESH,
        )

    load_i = pltpu.make_async_copy(integrals_hbm, ints, load_sem.at[0])
    load_b = pltpu.make_async_copy(basis_hbm, basis, load_sem.at[1])

    def c_rows(s):
        return c_all.at[pl.ds(pl.multiple_of(s * o, o), o), :]

    load_c = pltpu.make_async_copy(core_hbm, c_rows(me), load_sem.at[2])
    load_c.start()
    load_i.start()
    load_b.start()

    barrier = pltpu.get_barrier_semaphore()
    pl.semaphore_signal(barrier, inc=1, device_id=(sib, z), device_id_type=MESH)
    for i in range(1, nc):
        pl.semaphore_signal(barrier, inc=1, device_id=(peer(i), z), device_id_type=MESH)
    for j in range(1, m):
        pl.semaphore_signal(
            barrier, inc=1, device_id=(me, lax.rem(z + j, m)), device_id_type=MESH
        )
    pl.semaphore_wait(barrier, nc + m - 1)

    def gather_start(slot, send, recv):
        for i in range(nc):
            to = sib if i == 0 else peer(i)
            rc(slot(me), slot(me), send.at[i], recv.at[me], to, z).start()

    def gather_forward(slot, fwd, recv):
        for i in range(1, nc):
            s = back(i)
            copy = rc(slot(s), slot(s), fwd.at[i], recv.at[s], sib, z)
            copy.wait_recv()
            copy.start()

    def gather_finish(slot, send, fwd, recv):
        for i in range(nc):
            s = other(i)
            rc(slot(s), slot(s), send.at[i], recv.at[s], sib, z).wait_recv()
        for i in range(nc):
            rc(slot(me), slot(me), send.at[i], recv.at[me], sib, z).wait_send()
            if i:
                rc(slot(me), slot(me), fwd.at[i], recv.at[me], sib, z).wait_send()

    load_c.wait()
    gather_start(c_rows, c_send, c_recv)

    load_i.wait()
    TA = 256
    eye = one_hot(TA, TA, lambda row: row)

    @pl.loop(0, A // TA)
    def _(t):
        at = pl.multiple_of(t * TA, TA)
        left[pl.ds(at, TA), :] = dot_nt(eye, ints[:, pl.ds(at, TA)]).astype(BF16)

    load_b.wait()
    TK = 128
    pick = one_hot(TK, TK * m, lambda row: (row // o) * blk + z * o + lax.rem(row, o))

    @pl.loop(0, K // TK)
    def _(t):
        kept = dot_nt(pick, basis[:, pl.ds(pl.multiple_of(t * TK * m, TK * m), TK * m)])
        left[pl.ds(pl.multiple_of(A + t * TK, TK), TK), :] = (kept * energies[...]).astype(BF16)

    def sib_copy(i):
        return rc(sib_out.at[i], sib_in.at[i], s_send.at[i], s_recv.at[i], sib, z)

    def peer_copy(i):
        return rc(summed.at[i], peer_in.at[i], x_send.at[i], x_recv.at[i], peer(i), z)

    def partial_block(pair, dst):
        col = pl.ds(pl.multiple_of(pair * blk, blk), blk)

        @pl.loop(0, 3)
        def _(t):
            rows = pl.ds(pl.multiple_of(t * TM, TM), TM)
            dst[rows, :] = dot_nn(left[rows, :], basis[:, col]).astype(BF16)

    def combine(i):
        sib_copy(i).wait_recv()

        @pl.loop(0, D // 128)
        def _(t):
            rows = pl.ds(pl.multiple_of(t * 128, 128), 128)
            summed[i, rows, :] = (
                summed[i, rows, :].astype(F32) + sib_in[i, rows, :].astype(F32)
            ).astype(BF16)

        peer_copy(i).start()

    order = list(range(nc - 1, 0, -1)) + [0]
    for k, i in enumerate(order):
        to = peer(i)
        partial_block(to + 1 - 2 * c, sib_out.at[i])
        sib_copy(i).start()
        if k >= 1:
            combine(order[k - 1])
        partial_block(to, summed.at[i])

    gather_forward(c_rows, c_fwd, c_recv)
    sib_copy(0).wait_recv()
    for i in range(1, nc):
        peer_copy(i).wait_recv()

    @pl.loop(0, D // 128)
    def _(t):
        rows = pl.ds(pl.multiple_of(t * 128, 128), 128)
        total = summed[0, rows, :].astype(F32) + sib_in[0, rows, :].astype(F32)
        for i in range(1, nc):
            total += peer_in[i, rows, :].astype(F32)
        final[rows, :] = total.astype(BF16)

    def p_slot(s):
        return p_all.at[s]

    p_all[me] = final[0:A, :]
    gather_start(p_slot, p_send, p_recv)
    final_t[...] = dot_nt(one_hot(blk, blk, lambda row: row), final[...]).astype(BF16)
    gather_finish(c_rows, c_send, c_fwd, c_recv)
    gather_forward(p_slot, p_fwd, p_recv)
    gather_finish(p_slot, p_send, p_fwd, p_recv)

    per = n // H

    def z_copy(h, j):
        zz = lax.rem(z + j, m)
        rows = pl.ds(pl.multiple_of(zz * o, o), o)
        return rc(term_b.at[h, rows, :], z_in.at[h, j], z_send.at[h, j], z_recv.at[h, j], me, zz)

    for h in range(H):
        @pl.loop(0, per)
        def _(k):
            q = h * per + k
            value = dot_nn(final_t[:, 0:A], p_all[q])
            value += dot_nn(
                final_t[:, A:D], c_all[:, pl.ds(pl.multiple_of(q * blk, blk), blk)]
            )
            col = pl.ds(pl.multiple_of(k * blk, blk), blk)
            term[h, :, col] = value
            term_b[h, :, col] = value.astype(BF16)

        for j in range(1, m):
            z_copy(h, j).start()

    own = me * m + z

    def slot(h, owner):
        return core_all.at[h, pl.ds(pl.multiple_of(owner * o, o), o), :]

    def core_copy(h, owner, ssem, pair, zz):
        return rc(slot(h, owner), slot(h, owner), ssem, g_recv.at[h, owner], pair, zz)

    def spread(h, j, owner):
        for i in range(1, nc):
            core_copy(h, owner, g_send.at[h, j, i], peer(i), z).start()
        core_copy(h, owner, g_send.at[h, j, 0], sib, z).start()

    for h in range(H):
        for j in range(1, m):
            z_copy(h, j).wait_recv()
        cols = pl.ds(h * w, w)
        total = term[h, pl.ds(pl.multiple_of(z * o, o), o), :]
        for j in range(1, m):
            total += z_in[h, j].astype(F32)
        current = c_all[pl.ds(pl.multiple_of(me * o, o), o), cols].astype(F32)
        value = current - total / (own_denoms[...] + denoms[:, cols])
        next_ref[:, cols] = value
        core_all[h, pl.ds(pl.multiple_of(own * o, o), o), :] = value.astype(BF16)
        for j in range(1, m):
            core_copy(h, own, zg_send.at[h, j], me, lax.rem(z + j, m)).start()
        spread(h, 0, own)

    for h in range(H):
        @pl.loop(1, m)
        def _(j):
            owner = me * m + lax.rem(z + m - j, m)
            core_copy(h, owner, g_send.at[h, j, 0], sib, z).wait_recv()
            spread(h, j, owner)

    TR, TN = 512, 256
    writes = []
    for h in range(H):
        @pl.loop(0, m)
        def _(j):
            for i in range(1, nc):
                owner = back(i) * m + lax.rem(z + m - j, m)
                copy = core_copy(h, owner, g_fwd.at[h, j, i], sib, z)
                copy.wait_recv()
                copy.start()

        @pl.loop(0, m)
        def _(j):
            for i in range(nc):
                owner = other(i) * m + lax.rem(z + m - j, m)
                core_copy(h, owner, g_send.at[h, j, i], sib, z).wait_recv()

        for t in range(S // TR):
            b = len(writes) % 2
            if len(writes) >= 2:
                writes[-2].wait()

            @pl.loop(0, w // TN)
            def _(k):
                col = pl.ds(pl.multiple_of(k * TN, TN), TN)
                stage[b, :, col] = dot_nn(
                    basis[t * TR:(t + 1) * TR, :], core_all[h, :, col]
                ).astype(BF16)

            copy = pltpu.make_async_copy(
                stage.at[b], amps_hbm.at[pl.ds(t * TR, TR), pl.ds(h * w, w)], out_sem.at[b]
            )
            copy.start()
            writes.append(copy)
    for copy in writes[-2:]:
        copy.wait()

    for i in range(nc):
        sib_copy(i).wait_send()
        if i:
            peer_copy(i).wait_send()
    for h in range(H):
        for j in range(1, m):
            z_copy(h, j).wait_send()
            core_copy(h, own, zg_send.at[h, j], sib, z).wait_send()

        @pl.loop(0, m)
        def _(j):
            for i in range(nc):
                core_copy(h, own, g_send.at[h, j, i], sib, z).wait_send()
                if i:
                    core_copy(h, own, g_fwd.at[h, j, i], sib, z).wait_send()


def local(basis_rows, energies, integrals, core_amps, denominators):
    n, m = lax.axis_size("pair"), lax.axis_size("cores")
    nc = n // 2
    S, R = basis_rows.shape
    A = integrals.shape[1]
    o = core_amps.shape[0]
    blk, K = o * m, o * n
    D = A + K
    H = 2
    w = R // H
    owner = lax.axis_index("pair") * m + lax.axis_index("cores")
    own_denoms = lax.dynamic_slice_in_dim(denominators, owner * o, o, 0)[:, None]
    dma = pltpu.SemaphoreType.DMA
    vmem = pl.BlockSpec(memory_space=pltpu.VMEM)
    anyspace = pl.BlockSpec(memory_space=pl.ANY)
    flops = 2 * S * R * (D + R)
    return pl.pallas_call(
        functools.partial(kernel, n, m, H),
        out_shape=(
            jax.ShapeDtypeStruct((o, R), F32),
            jax.ShapeDtypeStruct((S, R), BF16),
        ),
        in_specs=[anyspace, vmem, anyspace, anyspace, vmem, vmem],
        out_specs=(vmem, anyspace),
        scratch_shapes=[
            pltpu.VMEM((S, R), BF16),
            pltpu.VMEM((S, A), BF16),
            pltpu.VMEM((D, S), BF16),
            pltpu.VMEM((nc, D, blk), BF16),
            pltpu.VMEM((nc, D, blk), BF16),
            pltpu.VMEM((nc, D, blk), BF16),
            pltpu.VMEM((nc, D, blk), BF16),
            pltpu.VMEM((D, blk), BF16),
            pltpu.VMEM((blk, D), BF16),
            pltpu.VMEM((n, A, blk), BF16),
            pltpu.VMEM((K, R), BF16),
            pltpu.VMEM((H, blk, w), F32),
            pltpu.VMEM((H, blk, w), BF16),
            pltpu.VMEM((H, m, o, w), BF16),
            pltpu.VMEM((H, R, w), BF16),
            pltpu.VMEM((2, 512, w), BF16),
            dma((3,)), dma((2,)),
            dma((nc,)), dma((nc,)), dma((n,)),
            dma((nc,)), dma((nc,)), dma((nc,)), dma((nc,)),
            dma((nc,)), dma((nc,)), dma((n,)),
            dma((H, m)), dma((H, m)), dma((H, m)),
            dma((H, m, nc)), dma((H, m, nc)), dma((H, n * m)),
        ],
        compiler_params=pltpu.CompilerParams(
            collective_id=0, has_side_effects=True, vmem_limit_bytes=60 * 2**20
        ),
        cost_estimate=pl.CostEstimate(
            flops=flops, bytes_accessed=2 * S * (2 * R + A), transcendentals=0
        ),
    )(basis_rows, energies[None, :], integrals, core_amps, own_denoms, denominators[None, :])


def solution(mesh):
    in_specs = (P("pair", None), P("pair"), P("pair", "cores"), P(("pair", "cores"), None), P())
    out_specs = (P(("pair", "cores"), None), P("pair", None))
    return jax.shard_map(local, mesh=mesh, in_specs=in_specs, out_specs=out_specs, check_vma=False)
```

```python
import functools

import jax
import jax.numpy as jnp
from jax import lax
from jax.experimental import pallas as pl
from jax.experimental.pallas import tpu as pltpu
from jax.sharding import PartitionSpec as P

F32 = jnp.float32
BF16 = jnp.bfloat16
MESH = pl.DeviceIdType.MESH


def dot_nn(left, right):
    return lax.dot_general(left, right, (((1,), (0,)), ((), ())), preferred_element_type=F32)


def dot_nt(left, right):
    return lax.dot_general(left, right, (((1,), (1,)), ((), ())), preferred_element_type=F32)


def one_hot(rows, columns, column_of):
    row = lax.broadcasted_iota(jnp.int32, (rows, columns), 0)
    column = lax.broadcasted_iota(jnp.int32, (rows, columns), 1)
    return jnp.where(column == column_of(row), 1.0, 0.0).astype(BF16)


def kernel(
    n, m, H,
    basis_hbm, energies, integrals_hbm, core_hbm, own_denoms, denoms,
    next_ref, amps_hbm,
    basis, ints, left, sib_out, sib_in, summed, peer_in, relay_in, final, final_t, p_all, c_all,
    term, term_b, z_in, core_all, stage,
    load_sem, out_sem, c_send, c_fwd, c_rel, c_recv, c_recv_d,
    s_send, s_recv, x_send, x_recv, y_send, y_recv,
    p_send, p_fwd, p_rel, p_recv, p_recv_d, z_send, z_recv,
    zg_send, g_send, g_fwd, g_rel, g_recv, g_recv_d,
):
    me, z = lax.axis_index("pair"), lax.axis_index("cores")
    nc = n // 2
    chip, c = me // 2, lax.rem(me, 2)
    sib = chip * 2 + 1 - c
    S, R = basis.shape
    A = ints.shape[1]
    K, blk = R // m, R // n
    o = blk // m
    w = R // H
    D = A + K
    TM = D // 2
    relay = nc == 4 and o % 32 == 0

    def chip_at(i, step):
        if not relay:
            return lax.rem(chip + (i if step > 0 else nc - i), nc)
        high, low = chip // 2, lax.rem(chip, 2)
        high = 1 - high if i // 2 else high
        low = 1 - low if i % 2 else low
        return high * 2 + low

    def peer(i):
        return chip_at(i, 1) * 2 + c

    def back(i):
        return chip_at(i, -1) * 2 + c

    def other(i):
        return chip_at(i, -1) * 2 + 1 - c

    def rc(src, dst, ssem, rsem, pair, zz):
        return pltpu.make_async_remote_copy(
            src_ref=src, dst_ref=dst, send_sem=ssem, recv_sem=rsem,
            device_id=(pair, zz), device_id_type=MESH,
        )

    load_i = pltpu.make_async_copy(integrals_hbm, ints, load_sem.at[0])
    load_b = pltpu.make_async_copy(basis_hbm, basis, load_sem.at[1])

    def c_rows(s, k=None):
        if k is None:
            return c_all.at[pl.ds(pl.multiple_of(s * o, o), o), :]
        part = o // 2
        return c_all.at[pl.ds(pl.multiple_of(s * o + k * part, part), part), :]

    load_c = pltpu.make_async_copy(core_hbm, c_rows(me), load_sem.at[2])
    load_c.start()
    load_i.start()
    load_b.start()

    barrier = pltpu.get_barrier_semaphore()
    pl.semaphore_signal(barrier, inc=1, device_id=(sib, z), device_id_type=MESH)
    for i in range(1, nc):
        pl.semaphore_signal(barrier, inc=1, device_id=(peer(i), z), device_id_type=MESH)
    for j in range(1, m):
        pl.semaphore_signal(
            barrier, inc=1, device_id=(me, lax.rem(z + j, m)), device_id_type=MESH
        )
    pl.semaphore_wait(barrier, nc + m - 1)

    def gather(slot, send, fwd, rel, recv, recv_d):
        near = [1, 2] if relay else list(range(1, nc))

        def start():
            for i in near + [0]:
                to = peer(i) if i else sib
                rc(slot(me), slot(me), send(i), recv(me), to, z).start()

        def half(s, k, to):
            return rc(slot(s, k), slot(s, k), rel(k), recv_d() if k else recv(s), to, z)

        def forward():
            for i in near:
                s = back(i)
                copy = rc(slot(s), slot(s), fwd(i), recv(s), sib, z)
                copy.wait_recv()
                if relay:
                    half(s, i - 1, peer(3 - i)).start()
                copy.start()

        def tail():
            if relay:
                s = back(3)
                half(s, 0, sib).wait_recv()
                half(s, 1, sib).wait_recv()
                rc(slot(s), slot(s), fwd(3), recv(s), sib, z).start()

        def other_arrived(i):
            s = other(i)
            rc(slot(s), slot(s), send(0), recv(s), sib, z).wait_recv()

        def sent():
            for i in near + [0]:
                rc(slot(me), slot(me), send(i), recv(me), sib, z).wait_send()
            for i in range(1, nc):
                rc(slot(me), slot(me), fwd(i), recv(me), sib, z).wait_send()
            if relay:
                half(me, 0, sib).wait_send()
                half(me, 1, sib).wait_send()

        return start, forward, tail, other_arrived, sent

    load_c.wait()
    c_start, c_forward, c_tail, c_other, c_sent = gather(
        c_rows, lambda i: c_send.at[i], lambda i: c_fwd.at[i], lambda k: c_rel.at[k],
        lambda s: c_recv.at[s], lambda: c_recv_d.at[0],
    )
    c_start()

    load_i.wait()
    TA = 256
    eye = one_hot(TA, TA, lambda row: row)

    @pl.loop(0, A // TA)
    def _(t):
        at = pl.multiple_of(t * TA, TA)
        left[pl.ds(at, TA), :] = dot_nt(eye, ints[:, pl.ds(at, TA)]).astype(BF16)

    load_b.wait()
    TK = 128
    pick = one_hot(TK, TK * m, lambda row: (row // o) * blk + z * o + lax.rem(row, o))

    @pl.loop(0, K // TK)
    def _(t):
        kept = dot_nt(pick, basis[:, pl.ds(pl.multiple_of(t * TK * m, TK * m), TK * m)])
        left[pl.ds(pl.multiple_of(A + t * TK, TK), TK), :] = (kept * energies[...]).astype(BF16)

    def sib_copy(i):
        return rc(sib_out.at[i], sib_in.at[i], s_send.at[i], s_recv.at[i], sib, z)

    def peer_copy(i):
        return rc(summed.at[i], peer_in.at[i], x_send.at[i], x_recv.at[i], peer(i), z)

    def partial_block(pair, dst):
        col = pl.ds(pl.multiple_of(pair * blk, blk), blk)

        @pl.loop(0, 2)
        def _(t):
            rows = pl.ds(pl.multiple_of(t * TM, TM), TM)
            dst[rows, :] = dot_nn(left[rows, :], basis[:, col]).astype(BF16)

    hd = D // 2

    def relay_copy(k):
        return rc(
            summed.at[3, pl.ds(k * hd, hd), :], relay_in.at[k],
            y_send.at[k], y_recv.at[k], peer(k + 1), z,
        )

    def combine(i):
        sib_copy(i).wait_recv()
        passed = None
        if relay and i < 3:
            passed = 2 - i
            relay_copy(passed).wait_recv()

        for k in range(2):
            @pl.loop(0, hd // 128)
            def _(t):
                at = pl.ds(pl.multiple_of(t * 128, 128), 128)
                rows = pl.ds(pl.multiple_of(k * hd + t * 128, 128), 128)
                value = summed[i, rows, :].astype(F32) + sib_in[i, rows, :].astype(F32)
                if passed == k:
                    value += relay_in[k, at, :].astype(F32)
                summed[i, rows, :] = value.astype(BF16)

        if relay and i == 3:
            relay_copy(0).start()
            relay_copy(1).start()
        else:
            peer_copy(i).start()

    def sib_part(i):
        partial_block(peer(i) + 1 - 2 * c, sib_out.at[i])
        sib_copy(i).start()

    def own_part(i):
        partial_block(peer(i), summed.at[i])

    if relay:
        sib_part(3)
        own_part(3)
        sib_part(1)
        combine(3)
        own_part(1)
        c_forward()
        sib_part(2)
        own_part(2)
        combine(1)
        sib_part(0)
        combine(2)
        own_part(0)
        c_tail()
    else:
        order = list(range(nc - 1, 0, -1)) + [0]
        for k, i in enumerate(order):
            sib_part(i)
            if k >= 1:
                combine(order[k - 1])
            own_part(i)
        c_forward()

    sib_copy(0).wait_recv()
    direct = [1, 2] if relay else list(range(1, nc))
    for i in direct:
        peer_copy(i).wait_recv()

    @pl.loop(0, D // 128)
    def _(t):
        rows = pl.ds(pl.multiple_of(t * 128, 128), 128)
        total = summed[0, rows, :].astype(F32) + sib_in[0, rows, :].astype(F32)
        for i in direct:
            total += peer_in[i, rows, :].astype(F32)
        final[rows, :] = total.astype(BF16)

    def p_slot(s, k=None):
        return p_all.at[s] if k is None else p_all.at[s, pl.ds(k * (A // 2), A // 2), :]

    p_all[me] = final[0:A, :]
    p_start, p_forward, p_tail, p_other, p_sent = gather(
        p_slot, lambda i: p_send.at[i], lambda i: p_fwd.at[i], lambda k: p_rel.at[k],
        lambda s: p_recv.at[s], lambda: p_recv_d.at[0],
    )
    p_start()
    final_t[...] = dot_nt(one_hot(blk, blk, lambda row: row), final[...]).astype(BF16)
    for i in range(nc):
        c_other(i)

    def z_copy(q, j):
        rows = pl.ds(pl.multiple_of(lax.rem(z + j, m) * o, o), o)
        return rc(
            term_b.at[q, rows, :], z_in.at[q, j], z_send.at[q, j], z_recv.at[q, j],
            me, lax.rem(z + j, m),
        )

    def add_term(q):
        value = dot_nn(final_t[:, 0:A], p_all[q])
        value += dot_nn(final_t[:, A:D], c_all[:, pl.ds(pl.multiple_of(q * blk, blk), blk)])
        term[q] = value
        term_b[q] = value.astype(BF16)
        for j in range(1, m):
            z_copy(q, j).start()

    add_term(me)
    p_other(0)
    add_term(sib)
    p_forward()
    for i in direct:
        add_term(back(i))
    for i in direct:
        p_other(i)
        add_term(other(i))
    p_tail()
    if relay:
        add_term(back(3))
        p_other(3)
        add_term(other(3))

    own = me * m + z

    def core_gather(h, j):
        zz = lax.rem(z + m - j, m)

        def slot(s, k=None):
            at = (s * m + zz) * o
            if k is None:
                return core_all.at[h, pl.ds(pl.multiple_of(at, o), o), :]
            part = o // 2
            return core_all.at[h, pl.ds(pl.multiple_of(at + k * part, part), part), :]

        return gather(
            slot, lambda i: g_send.at[h, j, i], lambda i: g_fwd.at[h, j, i],
            lambda k: g_rel.at[h, j, k], lambda s: g_recv.at[h, s * m + zz],
            lambda: g_recv_d.at[h, j],
        )

    def along_z(h, j, owner):
        rows = core_all.at[h, pl.ds(pl.multiple_of(owner * o, o), o), :]
        return rc(rows, rows, zg_send.at[h, j], g_recv.at[h, owner], me, lax.rem(z + j, m))

    per = n // H
    for h in range(H):
        for k in range(per):
            q = h * per + k
            for j in range(1, m):
                z_copy(q, j).wait_recv()
            cols = pl.ds(q * blk, blk)
            total = term[q, pl.ds(pl.multiple_of(z * o, o), o), :]
            for j in range(1, m):
                total += z_in[q, j].astype(F32)
            current = c_all[pl.ds(pl.multiple_of(me * o, o), o), cols].astype(F32)
            value = current - total / (own_denoms[...] + denoms[:, cols])
            next_ref[:, cols] = value
            core_all[h, pl.ds(pl.multiple_of(own * o, o), o), k * blk:(k + 1) * blk] = (
                value.astype(BF16)
            )
        for j in range(1, m):
            along_z(h, j, own).start()
        core_gather(h, 0)[0]()

    def each_z(step, h, first=0):
        @pl.loop(first, m)
        def _(j):
            core_gather(h, j)[step]()

    def from_z(h):
        @pl.loop(1, m)
        def _(j):
            along_z(h, 1, me * m + lax.rem(z + m - j, m)).wait_recv()
            core_gather(h, j)[0]()

    TR, TN = 1024, 256
    writes = []

    def rows_of(h):
        @pl.loop(0, m)
        def _(j):
            for i in range(nc):
                core_gather(h, j)[3](i)

        for t in range(S // TR):
            b = len(writes) % 2
            if len(writes) >= 2:
                writes[-2].wait()

            @pl.loop(0, w // TN)
            def _(k):
                col = pl.ds(pl.multiple_of(k * TN, TN), TN)
                stage[b, :, col] = dot_nn(
                    basis[t * TR:(t + 1) * TR, :], core_all[h, :, col]
                ).astype(BF16)

            copy = pltpu.make_async_copy(
                stage.at[b], amps_hbm.at[pl.ds(t * TR, TR), pl.ds(h * w, w)], out_sem.at[b]
            )
            copy.start()
            writes.append(copy)

    for step in range(H + 3):
        if step < H:
            from_z(step)
        if 0 <= step - 1 < H:
            each_z(1, step - 1)
        if 0 <= step - 2 < H:
            each_z(2, step - 2)
        if 0 <= step - 3 < H:
            rows_of(step - 3)
    for copy in writes[-2:]:
        copy.wait()

    c_sent()
    p_sent()
    for i in range(nc):
        sib_copy(i).wait_send()
    for i in direct:
        peer_copy(i).wait_send()
    if relay:
        relay_copy(0).wait_send()
        relay_copy(1).wait_send()

    @pl.loop(0, n)
    def _(q):
        for j in range(1, m):
            z_copy(q, j).wait_send()

    for h in range(H):
        for j in range(1, m):
            along_z(h, j, own).wait_send()
        each_z(4, h)


def local(basis_rows, energies, integrals, core_amps, denominators):
    n, m = lax.axis_size("pair"), lax.axis_size("cores")
    nc = n // 2
    S, R = basis_rows.shape
    A = integrals.shape[1]
    o = core_amps.shape[0]
    blk, K = o * m, o * n
    D = A + K
    H = 4
    w = R // H
    owner = lax.axis_index("pair") * m + lax.axis_index("cores")
    own_denoms = lax.dynamic_slice_in_dim(denominators, owner * o, o, 0)[:, None]
    dma = pltpu.SemaphoreType.DMA
    vmem = pl.BlockSpec(memory_space=pltpu.VMEM)
    anyspace = pl.BlockSpec(memory_space=pl.ANY)
    flops = 2 * S * R * (D + R)
    return pl.pallas_call(
        functools.partial(kernel, n, m, H),
        out_shape=(
            jax.ShapeDtypeStruct((o, R), F32),
            jax.ShapeDtypeStruct((S, R), BF16),
        ),
        in_specs=[anyspace, vmem, anyspace, anyspace, vmem, vmem],
        out_specs=(vmem, anyspace),
        scratch_shapes=[
            pltpu.VMEM((S, R), BF16),
            pltpu.VMEM((S, A), BF16),
            pltpu.VMEM((D, S), BF16),
            pltpu.VMEM((nc, D, blk), BF16),
            pltpu.VMEM((nc, D, blk), BF16),
            pltpu.VMEM((nc, D, blk), BF16),
            pltpu.VMEM((nc, D, blk), BF16),
            pltpu.VMEM((2, D // 2, blk), BF16),
            pltpu.VMEM((D, blk), BF16),
            pltpu.VMEM((blk, D), BF16),
            pltpu.VMEM((n, A, blk), BF16),
            pltpu.VMEM((K, R), BF16),
            pltpu.VMEM((n, blk, blk), F32),
            pltpu.VMEM((n, blk, blk), BF16),
            pltpu.VMEM((n, m, o, blk), BF16),
            pltpu.VMEM((H, R, w), BF16),
            pltpu.VMEM((2, 1024, w), BF16),
            dma((3,)), dma((2,)),
            dma((nc,)), dma((nc,)), dma((2,)), dma((n,)), dma((1,)),
            dma((nc,)), dma((nc,)), dma((nc,)), dma((nc,)), dma((2,)), dma((2,)),
            dma((nc,)), dma((nc,)), dma((2,)), dma((n,)), dma((1,)), dma((n, m)), dma((n, m)),
            dma((H, m)), dma((H, m, nc)), dma((H, m, nc)), dma((H, m, 2)),
            dma((H, n * m)), dma((H, m)),
        ],
        compiler_params=pltpu.CompilerParams(
            collective_id=0, has_side_effects=True, vmem_limit_bytes=60 * 2**20
        ),
        cost_estimate=pl.CostEstimate(
            flops=flops, bytes_accessed=2 * S * (2 * R + A), transcendentals=0
        ),
    )(basis_rows, energies[None, :], integrals, core_amps, own_denoms, denominators[None, :])


def solution(mesh):
    in_specs = (P("pair", None), P("pair"), P("pair", "cores"), P(("pair", "cores"), None), P())
    out_specs = (P(("pair", "cores"), None), P("pair", None))
    return jax.shard_map(local, mesh=mesh, in_specs=in_specs, out_specs=out_specs, check_vma=False)
```

```python
import functools

import jax
import jax.numpy as jnp
from jax import lax
from jax.experimental import pallas as pl
from jax.experimental.pallas import tpu as pltpu
from jax.sharding import PartitionSpec as P

F32 = jnp.float32
BF16 = jnp.bfloat16
MESH = pl.DeviceIdType.MESH


def dot_nn(left, right):
    return lax.dot_general(left, right, (((1,), (0,)), ((), ())), preferred_element_type=F32)


def dot_nt(left, right):
    return lax.dot_general(left, right, (((1,), (1,)), ((), ())), preferred_element_type=F32)


def one_hot(rows, columns, column_of):
    row = lax.broadcasted_iota(jnp.int32, (rows, columns), 0)
    column = lax.broadcasted_iota(jnp.int32, (rows, columns), 1)
    return jnp.where(column == column_of(row), 1.0, 0.0).astype(BF16)


def kernel(
    n, m, H,
    basis_hbm, energies, integrals_hbm, core_hbm, own_denoms, denoms,
    next_ref, amps_hbm,
    basis, ints, left, sib_out, sib_in, summed, peer_in, relay_in, final, final_t, p_all, c_all,
    term, term_b, z_in, core_all, stage,
    load_sem, out_sem, c_send, c_fwd, c_rel, c_recv, c_recv_d,
    s_send, s_recv, x_send, x_recv, y_send, y_recv,
    p_send, p_fwd, p_rel, p_recv, p_recv_d, z_send, z_recv,
    zg_send, g_send, g_fwd, g_rel, g_recv, g_recv_d,
):
    me, z = lax.axis_index("pair"), lax.axis_index("cores")
    nc = n // 2
    chip, c = me // 2, lax.rem(me, 2)
    sib = chip * 2 + 1 - c
    S, R = basis.shape
    A = ints.shape[1]
    K, blk = R // m, R // n
    o = blk // m
    w = R // H
    D = A + K
    TM = D // 2
    relay = nc == 4 and o % 32 == 0

    def chip_at(i, step):
        if not relay:
            return lax.rem(chip + (i if step > 0 else nc - i), nc)
        high, low = chip // 2, lax.rem(chip, 2)
        high = 1 - high if i // 2 else high
        low = 1 - low if i % 2 else low
        return high * 2 + low

    def peer(i):
        return chip_at(i, 1) * 2 + c

    def back(i):
        return chip_at(i, -1) * 2 + c

    def other(i):
        return chip_at(i, -1) * 2 + 1 - c

    def rc(src, dst, ssem, rsem, pair, zz):
        return pltpu.make_async_remote_copy(
            src_ref=src, dst_ref=dst, send_sem=ssem, recv_sem=rsem,
            device_id=(pair, zz), device_id_type=MESH,
        )

    load_i = pltpu.make_async_copy(integrals_hbm, ints, load_sem.at[0])
    load_b = pltpu.make_async_copy(basis_hbm, basis, load_sem.at[1])

    def c_rows(s, k=None):
        if k is None:
            return c_all.at[pl.ds(pl.multiple_of(s * o, o), o), :]
        part = o // 2
        return c_all.at[pl.ds(pl.multiple_of(s * o + k * part, part), part), :]

    load_c = pltpu.make_async_copy(core_hbm, c_rows(me), load_sem.at[2])
    load_c.start()
    load_i.start()
    load_b.start()

    barrier = pltpu.get_barrier_semaphore()
    pl.semaphore_signal(barrier, inc=1, device_id=(sib, z), device_id_type=MESH)
    for i in range(1, nc):
        pl.semaphore_signal(barrier, inc=1, device_id=(peer(i), z), device_id_type=MESH)
    for j in range(1, m):
        pl.semaphore_signal(
            barrier, inc=1, device_id=(me, lax.rem(z + j, m)), device_id_type=MESH
        )
    pl.semaphore_wait(barrier, nc + m - 1)

    def gather(slot, send, fwd, rel, recv, recv_d):
        near = [1, 2] if relay else list(range(1, nc))

        def start():
            for i in near + [0]:
                to = peer(i) if i else sib
                rc(slot(me), slot(me), send(i), recv(me), to, z).start()

        def half(s, k, to):
            return rc(slot(s, k), slot(s, k), rel(k), recv_d() if k else recv(s), to, z)

        def forward():
            for i in near:
                s = back(i)
                copy = rc(slot(s), slot(s), fwd(i), recv(s), sib, z)
                copy.wait_recv()
                if relay:
                    half(s, i - 1, peer(3 - i)).start()
                copy.start()

        def tail():
            if relay:
                s = back(3)
                half(s, 0, sib).wait_recv()
                half(s, 1, sib).wait_recv()
                rc(slot(s), slot(s), fwd(3), recv(s), sib, z).start()

        def other_arrived(i):
            s = other(i)
            rc(slot(s), slot(s), send(0), recv(s), sib, z).wait_recv()

        def sent():
            for i in near + [0]:
                rc(slot(me), slot(me), send(i), recv(me), sib, z).wait_send()
            for i in range(1, nc):
                rc(slot(me), slot(me), fwd(i), recv(me), sib, z).wait_send()
            if relay:
                half(me, 0, sib).wait_send()
                half(me, 1, sib).wait_send()

        return start, forward, tail, other_arrived, sent

    load_c.wait()
    c_start, c_forward, c_tail, c_other, c_sent = gather(
        c_rows, lambda i: c_send.at[i], lambda i: c_fwd.at[i], lambda k: c_rel.at[k],
        lambda s: c_recv.at[s], lambda: c_recv_d.at[0],
    )
    c_start()

    load_i.wait()
    TA = 256
    eye = one_hot(TA, TA, lambda row: row)

    @pl.loop(0, A // TA)
    def _(t):
        at = pl.multiple_of(t * TA, TA)
        left[pl.ds(at, TA), :] = dot_nt(eye, ints[:, pl.ds(at, TA)]).astype(BF16)

    load_b.wait()
    TK = 128
    pick = one_hot(TK, TK * m, lambda row: (row // o) * blk + z * o + lax.rem(row, o))

    @pl.loop(0, K // TK)
    def _(t):
        kept = dot_nt(pick, basis[:, pl.ds(pl.multiple_of(t * TK * m, TK * m), TK * m)])
        left[pl.ds(pl.multiple_of(A + t * TK, TK), TK), :] = (kept * energies[...]).astype(BF16)

    def sib_copy(i):
        return rc(sib_out.at[i], sib_in.at[i], s_send.at[i], s_recv.at[i], sib, z)

    def peer_copy(i):
        return rc(summed.at[i], peer_in.at[i], x_send.at[i], x_recv.at[i], peer(i), z)

    def partial_block(pair, dst):
        col = pl.ds(pl.multiple_of(pair * blk, blk), blk)

        @pl.loop(0, 2)
        def _(t):
            rows = pl.ds(pl.multiple_of(t * TM, TM), TM)
            dst[rows, :] = dot_nn(left[rows, :], basis[:, col]).astype(BF16)

    hd = D // 2

    def relay_copy(k):
        return rc(
            summed.at[3, pl.ds(k * hd, hd), :], relay_in.at[k],
            y_send.at[k], y_recv.at[k], peer(k + 1), z,
        )

    def combine(i):
        sib_copy(i).wait_recv()
        passed = None
        if relay and i < 3:
            passed = 2 - i
            relay_copy(passed).wait_recv()

        for k in range(2):
            @pl.loop(0, hd // 128)
            def _(t):
                at = pl.ds(pl.multiple_of(t * 128, 128), 128)
                rows = pl.ds(pl.multiple_of(k * hd + t * 128, 128), 128)
                value = summed[i, rows, :].astype(F32) + sib_in[i, rows, :].astype(F32)
                if passed == k:
                    value += relay_in[k, at, :].astype(F32)
                summed[i, rows, :] = value.astype(BF16)

        if relay and i == 3:
            relay_copy(0).start()
            relay_copy(1).start()
        else:
            peer_copy(i).start()

    def sib_part(i):
        partial_block(peer(i) + 1 - 2 * c, sib_out.at[i])
        sib_copy(i).start()

    def own_part(i):
        partial_block(peer(i), summed.at[i])

    if relay:
        sib_part(3)
        own_part(3)
        sib_part(1)
        combine(3)
        own_part(1)
        c_forward()
        sib_part(2)
        own_part(2)
        combine(1)
        sib_part(0)
        combine(2)
        own_part(0)
        c_tail()
    else:
        order = list(range(nc - 1, 0, -1)) + [0]
        for k, i in enumerate(order):
            sib_part(i)
            if k >= 1:
                combine(order[k - 1])
            own_part(i)
        c_forward()

    sib_copy(0).wait_recv()
    direct = [1, 2] if relay else list(range(1, nc))
    for i in direct:
        peer_copy(i).wait_recv()

    @pl.loop(0, D // 128)
    def _(t):
        rows = pl.ds(pl.multiple_of(t * 128, 128), 128)
        total = summed[0, rows, :].astype(F32) + sib_in[0, rows, :].astype(F32)
        for i in direct:
            total += peer_in[i, rows, :].astype(F32)
        final[rows, :] = total.astype(BF16)

    def p_slot(s, k=None):
        return p_all.at[s] if k is None else p_all.at[s, pl.ds(k * (A // 2), A // 2), :]

    p_all[me] = final[0:A, :]
    p_start, p_forward, p_tail, p_other, p_sent = gather(
        p_slot, lambda i: p_send.at[i], lambda i: p_fwd.at[i], lambda k: p_rel.at[k],
        lambda s: p_recv.at[s], lambda: p_recv_d.at[0],
    )
    p_start()
    final_t[...] = dot_nt(one_hot(blk, blk, lambda row: row), final[...]).astype(BF16)
    for i in range(nc):
        c_other(i)

    def z_copy(q, j):
        rows = pl.ds(pl.multiple_of(lax.rem(z + j, m) * o, o), o)
        return rc(
            term_b.at[q, rows, :], z_in.at[q, j], z_send.at[q, j], z_recv.at[q, j],
            me, lax.rem(z + j, m),
        )

    def add_term(q):
        value = dot_nn(final_t[:, 0:A], p_all[q])
        value += dot_nn(final_t[:, A:D], c_all[:, pl.ds(pl.multiple_of(q * blk, blk), blk)])
        term[q] = value
        term_b[q] = value.astype(BF16)
        for j in range(1, m):
            z_copy(q, j).start()

    add_term(me)
    p_other(0)
    add_term(sib)
    p_forward()
    for i in direct:
        add_term(back(i))
    for i in direct:
        p_other(i)
        add_term(other(i))
    p_tail()
    if relay:
        add_term(back(3))
        p_other(3)
        add_term(other(3))

    own = me * m + z

    def core_gather(h, j):
        zz = lax.rem(z + m - j, m)

        def slot(s, k=None):
            at = (s * m + zz) * o
            if k is None:
                return core_all.at[h, pl.ds(pl.multiple_of(at, o), o), :]
            part = o // 2
            return core_all.at[h, pl.ds(pl.multiple_of(at + k * part, part), part), :]

        return gather(
            slot, lambda i: g_send.at[h, j, i], lambda i: g_fwd.at[h, j, i],
            lambda k: g_rel.at[h, j, k], lambda s: g_recv.at[h, s * m + zz],
            lambda: g_recv_d.at[h, j],
        )

    def along_z(h, j, owner):
        rows = core_all.at[h, pl.ds(pl.multiple_of(owner * o, o), o), :]
        return rc(rows, rows, zg_send.at[h, j], g_recv.at[h, owner], me, lax.rem(z + j, m))

    per = n // H
    for h in range(H):
        for k in range(per):
            q = h * per + k
            for j in range(1, m):
                z_copy(q, j).wait_recv()
            cols = pl.ds(q * blk, blk)
            total = term[q, pl.ds(pl.multiple_of(z * o, o), o), :]
            for j in range(1, m):
                total += z_in[q, j].astype(F32)
            current = c_all[pl.ds(pl.multiple_of(me * o, o), o), cols].astype(F32)
            value = current - total / (own_denoms[...] + denoms[:, cols])
            next_ref[:, cols] = value
            core_all[h, pl.ds(pl.multiple_of(own * o, o), o), k * blk:(k + 1) * blk] = (
                value.astype(BF16)
            )
        for j in range(1, m):
            along_z(h, j, own).start()
        core_gather(h, 0)[0]()

    def each_z(step, h, first=0):
        @pl.loop(first, m)
        def _(j):
            core_gather(h, j)[step]()

    def from_z(h):
        @pl.loop(1, m)
        def _(j):
            along_z(h, 1, me * m + lax.rem(z + m - j, m)).wait_recv()
            core_gather(h, j)[0]()

    TR, TN = 1024, 256
    writes = []

    def rows_of(h):
        @pl.loop(0, m)
        def _(j):
            for i in range(nc):
                core_gather(h, j)[3](i)

        for t in range(S // TR):
            b = len(writes) % 2
            if len(writes) >= 2:
                writes[-2].wait()

            @pl.loop(0, w // TN)
            def _(k):
                col = pl.ds(pl.multiple_of(k * TN, TN), TN)
                stage[b, :, col] = dot_nn(
                    basis[t * TR:(t + 1) * TR, :], core_all[h, :, col]
                ).astype(BF16)

            copy = pltpu.make_async_copy(
                stage.at[b], amps_hbm.at[pl.ds(t * TR, TR), pl.ds(h * w, w)], out_sem.at[b]
            )
            copy.start()
            writes.append(copy)

    for step in range(H + 3):
        if step < H:
            from_z(step)
        if 0 <= step - 1 < H:
            each_z(1, step - 1)
        if 0 <= step - 2 < H:
            each_z(2, step - 2)
        if 0 <= step - 3 < H:
            rows_of(step - 3)
    for copy in writes[-2:]:
        copy.wait()

    c_sent()
    p_sent()
    for i in range(nc):
        sib_copy(i).wait_send()
    for i in direct:
        peer_copy(i).wait_send()
    if relay:
        relay_copy(0).wait_send()
        relay_copy(1).wait_send()

    @pl.loop(0, n)
    def _(q):
        for j in range(1, m):
            z_copy(q, j).wait_send()

    for h in range(H):
        for j in range(1, m):
            along_z(h, j, own).wait_send()
        each_z(4, h)


def local(basis_rows, energies, integrals, core_amps, denominators):
    n, m = lax.axis_size("pair"), lax.axis_size("cores")
    nc = n // 2
    S, R = basis_rows.shape
    A = integrals.shape[1]
    o = core_amps.shape[0]
    blk, K = o * m, o * n
    D = A + K
    H = 2
    w = R // H
    owner = lax.axis_index("pair") * m + lax.axis_index("cores")
    own_denoms = lax.dynamic_slice_in_dim(denominators, owner * o, o, 0)[:, None]
    dma = pltpu.SemaphoreType.DMA
    vmem = pl.BlockSpec(memory_space=pltpu.VMEM)
    anyspace = pl.BlockSpec(memory_space=pl.ANY)
    flops = 2 * S * R * (D + R)
    return pl.pallas_call(
        functools.partial(kernel, n, m, H),
        out_shape=(
            jax.ShapeDtypeStruct((o, R), F32),
            jax.ShapeDtypeStruct((S, R), BF16),
        ),
        in_specs=[anyspace, vmem, anyspace, anyspace, vmem, vmem],
        out_specs=(vmem, anyspace),
        scratch_shapes=[
            pltpu.VMEM((S, R), BF16),
            pltpu.VMEM((S, A), BF16),
            pltpu.VMEM((D, S), BF16),
            pltpu.VMEM((nc, D, blk), BF16),
            pltpu.VMEM((nc, D, blk), BF16),
            pltpu.VMEM((nc, D, blk), BF16),
            pltpu.VMEM((nc, D, blk), BF16),
            pltpu.VMEM((2, D // 2, blk), BF16),
            pltpu.VMEM((D, blk), BF16),
            pltpu.VMEM((blk, D), BF16),
            pltpu.VMEM((n, A, blk), BF16),
            pltpu.VMEM((K, R), BF16),
            pltpu.VMEM((n, blk, blk), F32),
            pltpu.VMEM((n, blk, blk), BF16),
            pltpu.VMEM((n, m, o, blk), BF16),
            pltpu.VMEM((H, R, w), BF16),
            pltpu.VMEM((2, 1024, w), BF16),
            dma((3,)), dma((2,)),
            dma((nc,)), dma((nc,)), dma((2,)), dma((n,)), dma((1,)),
            dma((nc,)), dma((nc,)), dma((nc,)), dma((nc,)), dma((2,)), dma((2,)),
            dma((nc,)), dma((nc,)), dma((2,)), dma((n,)), dma((1,)), dma((n, m)), dma((n, m)),
            dma((H, m)), dma((H, m, nc)), dma((H, m, nc)), dma((H, m, 2)),
            dma((H, n * m)), dma((H, m)),
        ],
        compiler_params=pltpu.CompilerParams(
            collective_id=0, has_side_effects=True, vmem_limit_bytes=60 * 2**20
        ),
        cost_estimate=pl.CostEstimate(
            flops=flops, bytes_accessed=2 * S * (2 * R + A), transcendentals=0
        ),
    )(basis_rows, energies[None, :], integrals, core_amps, own_denoms, denominators[None, :])


def solution(mesh):
    in_specs = (P("pair", None), P("pair"), P("pair", "cores"), P(("pair", "cores"), None), P())
    out_specs = (P(("pair", "cores"), None), P("pair", None))
    return jax.shard_map(local, mesh=mesh, in_specs=in_specs, out_specs=out_specs, check_vma=False)
```
